32 devices in a mesh: gx: 8 (over z, x), gy: 4 (over y, core).
Axes of the slice: x: 2, y: 2, z: 4, core: 2. Of those that a mesh axis runs over, the one named last changes fastest.
Arguments:
- base_flow: float32 [3, 192, 32, 1024], P(None, 'gx', None, 'gy'), may hold values from -6 to 6
- adjoint: float32 [3, 192, 32, 1024], P(None, 'gx', None, 'gy'), may hold values from -6 to 6
- first_op: bfloat16 [1024, 1024], replicated, may hold values from -2 to 2
- second_op: bfloat16 [1024, 1024], replicated, may hold values from -9 to 5
Outputs:
- new_adjoint: float32 [3, 192, 32, 1024], P(None, 'gx', None, 'gy')
The draws below stay inside these ranges and needn't reach their ends.
All inputs are finite; a program needn't handle non-finite values.
Results may differ from the reference program's by a relative error of at most 0.0025.
Values may be sent and summed in bfloat16 or wider, within the bound.
A program may use at most 128 MiB of HBM per device.

```python
import jax
import jax.numpy as jnp
from jax import lax

NY = 1024
NZ = 32
NX = 192


def grid_metric(key):
    metric_key = jax.random.fold_in(key, 7)
    return jnp.exp(jax.random.uniform(metric_key, (NY, 1), jnp.float32, -0.7, 0.7))


def operator_jitter(key, salt):
    jitter_key = jax.random.fold_in(key, salt)
    jitter = jnp.clip(jax.random.normal(jitter_key, (NY, NY), jnp.float32), -4.0, 4.0)
    return 0.3 * jitter / jnp.sqrt(jnp.float32(NY))


def draw_first_op(key, part):
    row_index = jnp.arange(NY)[:, None]
    col_index = jnp.arange(NY)[None, :]
    distance = jnp.abs(col_index - row_index).astype(jnp.float32)
    signed = jnp.sign(col_index - row_index).astype(jnp.float32)
    banded = signed * 0.8 * jnp.power(jnp.float32(0.3), distance - 1.0)
    metric = grid_metric(key)
    return (metric * (banded + operator_jitter(key, 1))).astype(jnp.bfloat16)


def draw_second_op(key, part):
    row_index = jnp.arange(NY)[:, None]
    col_index = jnp.arange(NY)[None, :]
    distance = jnp.abs(col_index - row_index).astype(jnp.float32)
    banded = jnp.where(distance == 0.0, -2.0, jnp.power(jnp.float32(0.35), jnp.maximum(distance - 1.0, 0.0)))
    metric = grid_metric(key)
    return (metric * metric * (banded + operator_jitter(key, 2))).astype(jnp.bfloat16)


def level_of(rng, dims, shards, low, largest):
    factor_of = 1.0
    for axis_at, shards_of in shards:
        steps = jax.random.uniform(jax.random.fold_in(jax.random.fold_in(rng, 6), axis_at), (shards_of,), jnp.float32, low / len(shards), largest / len(shards))
        factor_of = factor_of * jnp.repeat(jnp.exp(steps), dims[axis_at] // shards_of).reshape((-1,) + (1,) * (len(dims) - 1 - axis_at))
    return factor_of


def gaussian(key, shape, deviation, bound, split=(), kind=jnp.bfloat16):
    values = jax.random.normal(key, shape, jnp.float32) * deviation
    if len(split) > 0:
        values = level_of(key, shape, split, -0.22, 0.18) * values
    return jnp.clip(values, min=-bound, max=bound).astype(kind)


def setup_inputs(seed: int = 0) -> dict:
    streams_of = jax.random.split(jax.random.key(seed), 5)
    base_flow = gaussian(streams_of[0], (3, NX, NZ, NY), 1.0, 6.0, ((1, 8), (3, 4)), jnp.float32)
    adjoint = gaussian(streams_of[1], (3, NX, NZ, NY), 1.0, 6.0, ((1, 8), (3, 4)), jnp.float32)
    first_op = draw_first_op(jax.random.fold_in(streams_of[4], 71), 0)
    second_op = draw_second_op(jax.random.fold_in(streams_of[4], 71), 0)
    return {"base_flow": base_flow, "adjoint": adjoint, "first_op": first_op, "second_op": second_op}


C_FIRST = (0.8, -0.2, 4.0 / 105.0, -1.0 / 280.0)
C_SECOND = (1.6, -0.2, 8.0 / 315.0, -1.0 / 560.0)
C_CENTER = -205.0 / 72.0
VISCOSITY = 0.1
STEP_WEIGHT = 0.5


def first_periodic(field, direction):
    result = C_FIRST[0] * (jnp.roll(field, -1, direction) - jnp.roll(field, 1, direction))
    for offset in range(2, 5):
        result = result + C_FIRST[offset - 1] * (jnp.roll(field, -offset, direction) - jnp.roll(field, offset, direction))
    return result


def second_periodic(field, direction):
    result = C_CENTER * field
    for offset in range(1, 5):
        result = result + C_SECOND[offset - 1] * (jnp.roll(field, -offset, direction) + jnp.roll(field, offset, direction))
    return result


def wall_operator(values, matrix):
    return jnp.einsum("fxzk,ik->fxzi", values.astype(jnp.float32), matrix.astype(jnp.float32), precision=lax.Precision.HIGHEST)


def wall_combine(normal_vel, slope_adj, curvature, adjoint_low, slope_base):
    wall_part = normal_vel[None] * slope_adj + VISCOSITY * curvature
    coupling = jnp.sum(adjoint_low * slope_base, axis=0)
    return wall_part.at[1].add(-coupling)


def reference(base_flow, adjoint, first_op, second_op):
    base_low = lax.optimization_barrier(base_flow.astype(jnp.bfloat16))
    adjoint_low = lax.optimization_barrier(adjoint.astype(jnp.bfloat16))
    wall_base = wall_operator(base_low, first_op)
    wall_adjoint = wall_operator(adjoint_low, first_op)
    wall_curv = wall_operator(adjoint_low, second_op)
    wall_part = wall_combine(base_low[1].astype(jnp.float32), wall_adjoint, wall_curv, adjoint_low.astype(jnp.float32), wall_base)
    dx_base = first_periodic(base_flow, 1)
    dz_base = first_periodic(base_flow, 2)
    dx_adj = first_periodic(adjoint, 1)
    dz_adj = first_periodic(adjoint, 2)
    dxx_adj = second_periodic(adjoint, 1)
    dzz_adj = second_periodic(adjoint, 2)
    tendency = base_flow[0][None] * dx_adj + base_flow[2][None] * dz_adj + VISCOSITY * (dxx_adj + dzz_adj) + wall_part
    tendency = tendency.at[0].add(-jnp.sum(adjoint * dx_base, axis=0))
    tendency = tendency.at[2].add(-jnp.sum(adjoint * dz_base, axis=0))
    updated = adjoint + STEP_WEIGHT * tendency
    wall_index = jnp.arange(NY, dtype=jnp.int32)
    interior = (wall_index > 0) & (wall_index < NY - 1)
    return jnp.where(interior, updated, jnp.float32(0.0))
```

```python
import functools

import jax
import jax.numpy as jnp
from jax import lax
from jax.experimental import pallas as pl
from jax.experimental.pallas import tpu as pltpu
from jax.sharding import PartitionSpec as P

C_FIRST = (0.8, -0.2, 4.0 / 105.0, -1.0 / 280.0)
C_SECOND = (1.6, -0.2, 8.0 / 315.0, -1.0 / 560.0)
C_CENTER = -205.0 / 72.0
VISCOSITY = 0.1
STEP_WEIGHT = 0.5
MESH = pl.DeviceIdType.MESH
WIDTH = 4
LANES = 128


def kernel(
    groups,
    ring,
    chunks,
    base_hbm,
    adjoint_hbm,
    first_hbm,
    second_hbm,
    out_ref,
    ext,
    low,
    lines,
    halo,
    first,
    second,
    back_out,
    back_in,
    in_sem,
    own_sem,
    halo_send,
    halo_recv,
    line_send,
    line_recv,
    back_send,
    back_recv,
):
    cells, span, rows = low.shape[1], low.shape[2], low.shape[3]
    share = cells // groups
    step = share // chunks
    me = lax.axis_index("gy")
    here = lax.axis_index("gx")
    right = lax.rem(here + 1, ring)
    left = lax.rem(here + ring - 1, ring)
    order = [2, 1, 3] if groups == 4 else list(range(1, groups))
    peers = {d: lax.rem(me + d, groups) for d in range(groups)}

    loads = [
        pltpu.make_async_copy(base_hbm, ext.at[0:3, WIDTH : WIDTH + cells], in_sem.at[0]),
        pltpu.make_async_copy(adjoint_hbm, ext.at[3:6, WIDTH : WIDTH + cells], in_sem.at[1]),
        pltpu.make_async_copy(first_hbm, first, in_sem.at[2]),
        pltpu.make_async_copy(second_hbm, second, in_sem.at[3]),
    ]
    for load in loads:
        load.start()

    barrier = pltpu.get_barrier_semaphore()
    for d in order:
        pl.semaphore_signal(barrier, inc=1, device_id={"gy": peers[d]}, device_id_type=MESH)
    for side in (left, right):
        pl.semaphore_signal(barrier, inc=1, device_id={"gx": side}, device_id_type=MESH)

    loads[0].wait()
    loads[1].wait()

    def cast(x, carry):
        low[:, pl.ds(x, 1)] = ext[:, pl.ds(x + WIDTH, 1)].astype(jnp.bfloat16)
        return carry

    lax.fori_loop(0, cells, cast, 0)

    pl.semaphore_wait(barrier, groups + 1)

    mine = pl.ds(pl.multiple_of(me * rows, rows), rows)

    def line_copy(c, d):
        return pltpu.make_async_remote_copy(
            src_ref=low.at[:, pl.ds(peers[d] * share + c * step, step)],
            dst_ref=lines.at[c, :, :, :, mine],
            send_sem=line_send.at[c, d],
            recv_sem=line_recv.at[c, d],
            device_id={"gy": peers[d]},
            device_id_type=MESH,
        )

    def own_copy(c):
        return pltpu.make_async_copy(
            low.at[:, pl.ds(me * share + c * step, step)],
            lines.at[c, :, :, :, mine],
            own_sem.at[c],
        )

    def back_copy(c, d):
        return pltpu.make_async_remote_copy(
            src_ref=back_out.at[c, d],
            dst_ref=back_in.at[c, me],
            send_sem=back_send.at[c, d],
            recv_sem=back_recv.at[c, d],
            device_id={"gy": peers[d]},
            device_id_type=MESH,
        )

    to_right = pltpu.make_async_remote_copy(
        src_ref=low.at[:, cells - WIDTH : cells],
        dst_ref=halo.at[0],
        send_sem=halo_send.at[0],
        recv_sem=halo_recv.at[0],
        device_id={"gx": right},
        device_id_type=MESH,
    )
    to_left = pltpu.make_async_remote_copy(
        src_ref=low.at[:, 0:WIDTH],
        dst_ref=halo.at[1],
        send_sem=halo_send.at[1],
        recv_sem=halo_recv.at[1],
        device_id={"gx": left},
        device_id_type=MESH,
    )
    for d in order:
        line_copy(0, d).start()
    to_right.start()
    to_left.start()
    for c in range(1, chunks):
        for d in order:
            line_copy(c, d).start()
    for c in range(chunks):
        own_copy(c).start()

    def derive(x, carry):
        for half in range(rows // LANES):
            cols = slice(half * LANES, (half + 1) * LANES)

            def plane(f, offset):
                return ext[f, x + (WIDTH + offset), :, cols]

            stream = plane(0, 0)
            across = plane(2, 0)
            couple_x = None
            couple_z = None
            parts = []
            for j in range(3):
                adj = plane(3 + j, 0)
                slope_x = None
                curve = (2.0 * C_CENTER) * adj
                slope_z = None
                base_x = None
                base_z = None
                field = plane(j, 0)
                for k in range(1, WIDTH + 1):
                    a_up, a_down = plane(3 + j, k), plane(3 + j, -k)
                    z_up = pltpu.roll(adj, span - k, 0)
                    z_down = pltpu.roll(adj, k, 0)
                    dx = C_FIRST[k - 1] * (a_up - a_down)
                    dz = C_FIRST[k - 1] * (z_up - z_down)
                    curve = curve + C_SECOND[k - 1] * ((a_up + a_down) + (z_up + z_down))
                    bx = C_FIRST[k - 1] * (plane(j, k) - plane(j, -k))
                    bz = C_FIRST[k - 1] * (
                        pltpu.roll(field, span - k, 0) - pltpu.roll(field, k, 0)
                    )
                    slope_x = dx if slope_x is None else slope_x + dx
                    slope_z = dz if slope_z is None else slope_z + dz
                    base_x = bx if base_x is None else base_x + bx
                    base_z = bz if base_z is None else base_z + bz
                base_x, base_z = adj * base_x, adj * base_z
                couple_x = base_x if couple_x is None else couple_x + base_x
                couple_z = base_z if couple_z is None else couple_z + base_z
                carried = stream * slope_x + across * slope_z + VISCOSITY * curve
                parts.append(adj + STEP_WEIGHT * carried)
            out_ref[0, x, :, cols] = parts[0] - STEP_WEIGHT * couple_x
            out_ref[1, x, :, cols] = parts[1]
            out_ref[2, x, :, cols] = parts[2] - STEP_WEIGHT * couple_z
        return carry

    lax.fori_loop(WIDTH, cells - WIDTH, derive, 0)

    to_right.wait()
    to_left.wait()

    def widen(k, carry):
        ext[:, pl.ds(k, 1)] = halo[0, :, pl.ds(k, 1)].astype(jnp.float32)
        ext[:, pl.ds(k + WIDTH + cells, 1)] = halo[1, :, pl.ds(k, 1)].astype(jnp.float32)
        return carry

    lax.fori_loop(0, WIDTH, widen, 0)

    def edge(k, carry):
        derive(k, 0)
        derive(k + cells - WIDTH, 0)
        return carry

    lax.fori_loop(0, WIDTH, edge, 0)

    loads[2].wait()
    loads[3].wait()

    tall = 6 * step * span
    contract = (((1,), (1,)), ((), ()))

    def wall(c, carry):
        own_copy(c).wait()
        for d in order:
            line_copy(c, d).wait_recv()
        for d in order + [0]:
            block = pl.ds(pl.multiple_of(peers[d] * rows, rows), rows)
            every = lines[c].reshape(tall, groups * rows)
            slopes = lax.dot_general(
                every, first[block, :], contract, preferred_element_type=jnp.float32
            ).reshape(6, step, span, rows)
            curves = lax.dot_general(
                every[tall // 2 :], second[block, :], contract, preferred_element_type=jnp.float32
            ).reshape(3, step, span, rows)
            there = lines[c, :, :, :, block].astype(jnp.float32)
            couple = there[3] * slopes[0] + there[4] * slopes[1] + there[5] * slopes[2]
            parts = [there[1] * slopes[3 + j] + VISCOSITY * curves[j] for j in range(3)]
            parts[1] = parts[1] - couple
            for j in range(3):
                value = parts[j].astype(jnp.bfloat16)
                if d == 0:
                    back_in[c, me, j] = value
                else:
                    back_out[c, d, j] = value
            if d != 0:
                back_copy(c, d).start()
        return carry

    lax.fori_loop(0, chunks, wall, 0)

    place = me * rows + lax.broadcasted_iota(jnp.int32, (span, rows), 1)
    inside = (place > 0) & (place < groups * rows - 1)

    def finish(c, carry):
        for d in order:
            back_copy(c, d).wait_recv()

        def add(t, carry):
            owner = t // step
            within = lax.rem(t, step)
            x = owner * share + c * step + within
            for j in range(3):
                value = out_ref[j, x] + STEP_WEIGHT * back_in[c, owner, j, within].astype(
                    jnp.float32
                )
                out_ref[j, x] = jnp.where(inside, value, 0.0)
            return carry

        return lax.fori_loop(0, groups * step, add, carry)

    lax.fori_loop(0, chunks, finish, 0)

    for c in range(chunks):
        for d in order:
            line_copy(c, d).wait_send()
            back_copy(c, d).wait_send()


def body(base_flow, adjoint, first_op, second_op):
    _, cells, span, rows = base_flow.shape
    groups = lax.axis_size("gy")
    ring = lax.axis_size("gx")
    share = cells // groups
    chunks = 3 if share % 3 == 0 else 1
    step = share // chunks
    total = groups * rows
    low = jnp.bfloat16
    dma = pltpu.SemaphoreType.DMA
    return pl.pallas_call(
        functools.partial(kernel, groups, ring, chunks),
        out_shape=jax.ShapeDtypeStruct(base_flow.shape, jnp.float32),
        in_specs=[pl.BlockSpec(memory_space=pl.ANY)] * 4,
        out_specs=pl.BlockSpec(memory_space=pltpu.VMEM),
        scratch_shapes=[
            pltpu.VMEM((6, cells + 2 * WIDTH, span, rows), jnp.float32),
            pltpu.VMEM((6, cells, span, rows), low),
            pltpu.VMEM((chunks, 6, step, span, total), low),
            pltpu.VMEM((2, 6, WIDTH, span, rows), low),
            pltpu.VMEM((total, total), low),
            pltpu.VMEM((total, total), low),
            pltpu.VMEM((chunks, groups, 3, step, span, rows), low),
            pltpu.VMEM((chunks, groups, 3, step, span, rows), low),
            dma((4,)),
            dma((chunks,)),
            dma((2,)),
            dma((2,)),
            dma((chunks, groups)),
            dma((chunks, groups)),
            dma((chunks, groups)),
            dma((chunks, groups)),
        ],
        compiler_params=pltpu.CompilerParams(
            collective_id=0, has_side_effects=True, vmem_limit_bytes=56 * 1024 * 1024
        ),
    )(base_flow, adjoint, first_op, second_op)


def solution(mesh):
    return jax.shard_map(
        body,
        mesh=mesh,
        in_specs=(P(None, "gx", None, "gy"), P(None, "gx", None, "gy"), P(), P()),
        out_specs=P(None, "gx", None, "gy"),
        check_vma=False,
    )
```

```python
import functools

import jax
import jax.numpy as jnp
from jax import lax
from jax.experimental import pallas as pl
from jax.experimental.pallas import tpu as pltpu
from jax.sharding import PartitionSpec as P

C_FIRST = (0.8, -0.2, 4.0 / 105.0, -1.0 / 280.0)
C_SECOND = (1.6, -0.2, 8.0 / 315.0, -1.0 / 560.0)
C_CENTER = -205.0 / 72.0
VISCOSITY = 0.1
STEP_WEIGHT = 0.5
MESH = pl.DeviceIdType.MESH
WIDTH = 4
LANES = 128


def kernel(
    groups,
    ring,
    base_hbm,
    adjoint_hbm,
    first_hbm,
    second_hbm,
    out_ref,
    ext,
    low,
    lines,
    base_lines,
    halo,
    first,
    second,
    chip_first,
    part_out,
    part_in,
    in_sem,
    own_sem,
    halo_send,
    halo_recv,
    line_send,
    line_recv,
):
    cells, span, rows = low.shape[1], low.shape[2], low.shape[3]
    step = WIDTH
    chunks = cells // step
    me = lax.axis_index("gy")
    here = lax.axis_index("gx")
    right = lax.rem(here + 1, ring)
    left = lax.rem(here + ring - 1, ring)
    core = lax.rem(me, 2)
    chip = me // 2
    sibling = me + 1 - 2 * core
    partner = lax.rem(me + 2, groups)

    def block_of(index, size):
        return pl.ds(pl.multiple_of(index * size, size), size)

    mine = block_of(me, rows)
    across_y = block_of(partner, rows)
    chip_columns = block_of(chip, 2 * rows)
    core_columns = block_of(core, rows)
    loads = [
        pltpu.make_async_copy(adjoint_hbm, ext.at[3:6, WIDTH : WIDTH + cells], in_sem.at[0]),
        pltpu.make_async_copy(base_hbm, ext.at[0:3, WIDTH : WIDTH + cells], in_sem.at[1]),
        pltpu.make_async_copy(first_hbm.at[mine], first, in_sem.at[2]),
        pltpu.make_async_copy(second_hbm.at[mine], second, in_sem.at[3]),
        pltpu.make_async_copy(
            first_hbm.at[mine, chip_columns], chip_first.at[0], in_sem.at[4]
        ),
        pltpu.make_async_copy(
            first_hbm.at[across_y, chip_columns], chip_first.at[1], in_sem.at[5]
        ),
    ]
    loads[0].start()
    barrier = pltpu.get_barrier_semaphore()
    for other in (partner, sibling):
        pl.semaphore_signal(barrier, inc=1, device_id={"gy": other}, device_id_type=MESH)
    for side in (left, right):
        pl.semaphore_signal(barrier, inc=1, device_id={"gx": side}, device_id_type=MESH)
    for load in loads[1:]:
        load.start()

    def remote(src, dst, kind, q, axis, target):
        return pltpu.make_async_remote_copy(
            src_ref=src,
            dst_ref=dst,
            send_sem=line_send.at[kind, q],
            recv_sem=line_recv.at[kind, q],
            device_id={axis: target},
            device_id_type=MESH,
        )

    def layers(q):
        return pl.ds(q * step, step)

    def to_partner(q):
        return remote(
            low.at[3:6, layers(q)], lines.at[:, layers(q), :, mine], 0, q, "gy", partner
        )

    def to_sibling(q):
        return remote(
            low.at[3:6, layers(q)], lines.at[:, layers(q), :, mine], 1, q, "gy", sibling
        )

    def base_to_sibling(q):
        return remote(
            low.at[0:3, layers(q)],
            base_lines.at[:, layers(q), :, core_columns],
            2,
            q,
            "gy",
            sibling,
        )

    def forward(q):
        block = lines.at[:, layers(q), :, across_y]
        return remote(block, block, 3, q, "gy", sibling)

    def part_copy(q):
        return remote(part_out.at[layers(q)], part_in.at[layers(q)], 4, q, "gy", partner)

    own_adjoint = pltpu.make_async_copy(low.at[3:6], lines.at[:, :, :, mine], own_sem.at[0])
    own_base = pltpu.make_async_copy(
        low.at[0:3], base_lines.at[:, :, :, core_columns], own_sem.at[1]
    )
    to_right = pltpu.make_async_remote_copy(
        src_ref=low.at[:, cells - WIDTH : cells],
        dst_ref=halo.at[0],
        send_sem=halo_send.at[0],
        recv_sem=halo_recv.at[0],
        device_id={"gx": right},
        device_id_type=MESH,
    )
    to_left = pltpu.make_async_remote_copy(
        src_ref=low.at[:, 0:WIDTH],
        dst_ref=halo.at[1],
        send_sem=halo_send.at[1],
        recv_sem=halo_recv.at[1],
        device_id={"gx": left},
        device_id_type=MESH,
    )
    order = list(range(1, chunks - 1)) + [0, chunks - 1]

    def cast(field, x):
        low[field : field + 3, pl.ds(x, 1)] = ext[
            field : field + 3, pl.ds(x + WIDTH, 1)
        ].astype(jnp.bfloat16)

    def cast_adjoint(x, carry):
        cast(3, x)
        return carry

    def cast_base(x, carry):
        cast(0, x)
        return carry

    loads[0].wait()
    first_step = order[0] * step
    lax.fori_loop(first_step, first_step + step, cast_adjoint, 0)
    pl.semaphore_wait(barrier, 4)
    to_partner(order[0]).start()
    lax.fori_loop(first_step + step, cells, cast_adjoint, 0)
    lax.fori_loop(0, first_step, cast_adjoint, 0)
    for q in order[1:]:
        to_partner(q).start()
    loads[1].wait()
    lax.fori_loop(0, cells, cast_base, 0)
    to_right.start()
    to_left.start()
    for q in order:
        to_sibling(q).start()
        base_to_sibling(q).start()
    own_adjoint.start()
    own_base.start()

    def derive(x, carry):
        for half in range(rows // LANES):
            cols = slice(half * LANES, (half + 1) * LANES)

            def plane(f, offset):
                return ext[f, x + (WIDTH + offset), :, cols]

            stream = plane(0, 0)
            across = plane(2, 0)
            couple_x = None
            couple_z = None
            parts = []
            for j in range(3):
                adj = plane(3 + j, 0)
                slope_x = None
                curve = (2.0 * C_CENTER) * adj
                slope_z = None
                base_x = None
                base_z = None
                field = plane(j, 0)
                for k in range(1, WIDTH + 1):
                    a_up, a_down = plane(3 + j, k), plane(3 + j, -k)
                    z_up = pltpu.roll(adj, span - k, 0)
                    z_down = pltpu.roll(adj, k, 0)
                    dx = C_FIRST[k - 1] * (a_up - a_down)
                    dz = C_FIRST[k - 1] * (z_up - z_down)
                    curve = curve + C_SECOND[k - 1] * ((a_up + a_down) + (z_up + z_down))
                    bx = C_FIRST[k - 1] * (plane(j, k) - plane(j, -k))
                    bz = C_FIRST[k - 1] * (
                        pltpu.roll(field, span - k, 0) - pltpu.roll(field, k, 0)
                    )
                    slope_x = dx if slope_x is None else slope_x + dx
                    slope_z = dz if slope_z is None else slope_z + dz
                    base_x = bx if base_x is None else base_x + bx
                    base_z = bz if base_z is None else base_z + bz
                base_x, base_z = adj * base_x, adj * base_z
                couple_x = base_x if couple_x is None else couple_x + base_x
                couple_z = base_z if couple_z is None else couple_z + base_z
                carried = stream * slope_x + across * slope_z + VISCOSITY * curve
                parts.append(adj + STEP_WEIGHT * carried)
            out_ref[0, x, :, cols] = parts[0] - STEP_WEIGHT * couple_x
            out_ref[1, x, :, cols] = parts[1]
            out_ref[2, x, :, cols] = parts[2] - STEP_WEIGHT * couple_z
        return carry

    tall = 3 * step * span
    contract = (((1,), (1,)), ((), ()))

    def product(values, matrix):
        return lax.dot_general(
            values.reshape(tall, values.shape[3]),
            matrix,
            contract,
            preferred_element_type=jnp.float32,
        ).reshape(3, step, span, rows)

    def couple(q, cols, which):
        slopes = product(base_lines[:, layers(q)], chip_first[which])
        there = lines[:, layers(q), :, cols].astype(jnp.float32)
        return there[0] * slopes[0] + there[1] * slopes[1] + there[2] * slopes[2]

    def advance(q):
        lax.fori_loop(q * step, q * step + step, derive, 0)
        base_to_sibling(q).wait_recv()
        to_partner(q).wait_recv()
        forward(q).start()
        part_out[layers(q)] = couple(q, across_y, 1).astype(jnp.bfloat16)
        part_copy(q).start()

    place = me * rows + lax.broadcasted_iota(jnp.int32, (step, span, rows), 2)
    inside = (place > 0) & (place < groups * rows - 1)

    def wall(q):
        to_sibling(q).wait_recv()
        forward(q).wait_recv()
        here_x = layers(q)
        slopes = product(lines[:, here_x], first[...])
        curves = product(lines[:, here_x], second[...])
        normal = low[1, here_x].astype(jnp.float32)
        own = couple(q, mine, 0)
        for j in range(3):
            part = normal * slopes[j] + VISCOSITY * curves[j]
            if j == 1:
                part = part - own
            value = out_ref[j, here_x] + STEP_WEIGHT * part
            out_ref[j, here_x] = value if j == 1 else jnp.where(inside, value, 0.0)

    def finish(q, carry):
        part_copy(q).wait_recv()
        value = out_ref[1, layers(q)] - STEP_WEIGHT * part_in[layers(q)].astype(jnp.float32)
        out_ref[1, layers(q)] = jnp.where(inside, value, 0.0)
        return carry

    for load in loads[2:]:
        load.wait()
    own_adjoint.wait()
    own_base.wait()
    advance(1)

    def interior(q, carry):
        advance(q)
        wall(q - 1)
        return carry

    lax.fori_loop(2, chunks - 1, interior, 0)

    to_right.wait()
    to_left.wait()

    def widen(k, carry):
        ext[:, pl.ds(k, 1)] = halo[0, :, pl.ds(k, 1)].astype(jnp.float32)
        ext[:, pl.ds(k + WIDTH + cells, 1)] = halo[1, :, pl.ds(k, 1)].astype(jnp.float32)
        return carry

    lax.fori_loop(0, WIDTH, widen, 0)

    def edges(k, carry):
        q = k * (chunks - 1)
        advance(q)
        wall((1 - k) * (chunks - 2))
        return carry

    lax.fori_loop(0, 2, edges, 0)
    wall(chunks - 1)
    lax.fori_loop(0, chunks, finish, 0)

    for q in range(chunks):
        for copy in (to_partner, to_sibling, base_to_sibling, forward, part_copy):
            copy(q).wait_send()


def body(base_flow, adjoint, first_op, second_op):
    _, cells, span, rows = base_flow.shape
    groups = lax.axis_size("gy")
    ring = lax.axis_size("gx")
    chunks = cells // WIDTH
    total = groups * rows
    low = jnp.bfloat16
    dma = pltpu.SemaphoreType.DMA
    return pl.pallas_call(
        functools.partial(kernel, groups, ring),
        out_shape=jax.ShapeDtypeStruct(base_flow.shape, jnp.float32),
        in_specs=[pl.BlockSpec(memory_space=pltpu.HBM)] * 4,
        out_specs=pl.BlockSpec(memory_space=pltpu.VMEM),
        scratch_shapes=[
            pltpu.VMEM((6, cells + 2 * WIDTH, span, rows), jnp.float32),
            pltpu.VMEM((6, cells, span, rows), low),
            pltpu.VMEM((3, cells, span, total), low),
            pltpu.VMEM((3, cells, span, 2 * rows), low),
            pltpu.VMEM((2, 6, WIDTH, span, rows), low),
            pltpu.VMEM((rows, total), low),
            pltpu.VMEM((rows, total), low),
            pltpu.VMEM((2, rows, 2 * rows), low),
            pltpu.VMEM((cells, span, rows), low),
            pltpu.VMEM((cells, span, rows), low),
            dma((6,)),
            dma((2,)),
            dma((2,)),
            dma((2,)),
            dma((5, chunks)),
            dma((5, chunks)),
        ],
        compiler_params=pltpu.CompilerParams(
            collective_id=0, has_side_effects=True, vmem_limit_bytes=54 * 1024 * 1024
        ),
    )(base_flow, adjoint, first_op, second_op)


def solution(mesh):
    return jax.shard_map(
        body,
        mesh=mesh,
        in_specs=(P(None, "gx", None, "gy"), P(None, "gx", None, "gy"), P(), P()),
        out_specs=P(None, "gx", None, "gy"),
        check_vma=False,
    )
```

```python
import functools

import jax
import jax.numpy as jnp
from jax import lax
from jax.experimental import pallas as pl
from jax.experimental.pallas import tpu as pltpu
from jax.sharding import PartitionSpec as P

C_FIRST = (0.8, -0.2, 4.0 / 105.0, -1.0 / 280.0)
C_SECOND = (1.6, -0.2, 8.0 / 315.0, -1.0 / 560.0)
C_CENTER = -205.0 / 72.0
VISCOSITY = 0.1
STEP_WEIGHT = 0.5
MESH = pl.DeviceIdType.MESH
WIDTH = 4
LANES = 128


def kernel(
    groups,
    ring,
    base_hbm,
    adjoint_hbm,
    first_hbm,
    second_hbm,
    out_hbm,
    out_ref,
    ext,
    low,
    lines,
    base_lines,
    halo,
    first,
    second,
    chip_first,
    part_out,
    part_in,
    in_sem,
    out_sem,
    own_sem,
    halo_send,
    halo_recv,
    line_send,
    line_recv,
):
    cells, span, rows = low.shape[1], low.shape[2], low.shape[3]
    step = WIDTH
    chunks = cells // step
    me = lax.axis_index("gy")
    here = lax.axis_index("gx")
    right = lax.rem(here + 1, ring)
    left = lax.rem(here + ring - 1, ring)
    core = lax.rem(me, 2)
    chip = me // 2
    sibling = me + 1 - 2 * core
    partner = lax.rem(me + 2, groups)

    def block_of(index, size):
        return pl.ds(pl.multiple_of(index * size, size), size)

    mine = block_of(me, rows)
    across_y = block_of(partner, rows)
    chip_columns = block_of(chip, 2 * rows)
    core_columns = block_of(core, rows)
    order = list(range(1, chunks - 1)) + [0, chunks - 1]
    adjoint_loads = [
        pltpu.make_async_copy(
            adjoint_hbm.at[:, q * step : (q + 1) * step],
            ext.at[3:6, WIDTH + q * step : WIDTH + (q + 1) * step],
            in_sem.at[5 + q],
        )
        for q in range(chunks)
    ]
    loads = [
        pltpu.make_async_copy(base_hbm, ext.at[0:3, WIDTH : WIDTH + cells], in_sem.at[0]),
        pltpu.make_async_copy(first_hbm.at[mine], first, in_sem.at[1]),
        pltpu.make_async_copy(second_hbm.at[mine], second, in_sem.at[2]),
        pltpu.make_async_copy(
            first_hbm.at[mine, chip_columns], chip_first.at[0], in_sem.at[3]
        ),
        pltpu.make_async_copy(
            first_hbm.at[across_y, chip_columns], chip_first.at[1], in_sem.at[4]
        ),
    ]
    barrier = pltpu.get_barrier_semaphore()
    for other in (partner, sibling):
        pl.semaphore_signal(barrier, inc=1, device_id={"gy": other}, device_id_type=MESH)
    for side in (left, right):
        pl.semaphore_signal(barrier, inc=1, device_id={"gx": side}, device_id_type=MESH)
    for q in order:
        adjoint_loads[q].start()

    def remote(src, dst, kind, q, axis, target):
        return pltpu.make_async_remote_copy(
            src_ref=src,
            dst_ref=dst,
            send_sem=line_send.at[kind, q],
            recv_sem=line_recv.at[kind, q],
            device_id={axis: target},
            device_id_type=MESH,
        )

    def layers(q):
        return pl.ds(q * step, step)

    def to_partner(q):
        return remote(
            low.at[3:6, layers(q)], lines.at[:, layers(q), :, mine], 0, q, "gy", partner
        )

    def to_sibling(q):
        return remote(
            low.at[3:6, layers(q)], lines.at[:, layers(q), :, mine], 1, q, "gy", sibling
        )

    def base_to_sibling(q):
        return remote(
            low.at[0:3, layers(q)],
            base_lines.at[:, layers(q), :, core_columns],
            2,
            q,
            "gy",
            sibling,
        )

    def forward(q):
        block = lines.at[:, layers(q), :, across_y]
        return remote(block, block, 3, q, "gy", sibling)

    def part_copy(q):
        return remote(part_out.at[layers(q)], part_in.at[layers(q)], 4, q, "gy", partner)

    own_adjoint = pltpu.make_async_copy(low.at[3:6], lines.at[:, :, :, mine], own_sem.at[0])
    own_base = pltpu.make_async_copy(
        low.at[0:3], base_lines.at[:, :, :, core_columns], own_sem.at[1]
    )
    to_right = pltpu.make_async_remote_copy(
        src_ref=low.at[:, cells - WIDTH : cells],
        dst_ref=halo.at[0],
        send_sem=halo_send.at[0],
        recv_sem=halo_recv.at[0],
        device_id={"gx": right},
        device_id_type=MESH,
    )
    to_left = pltpu.make_async_remote_copy(
        src_ref=low.at[:, 0:WIDTH],
        dst_ref=halo.at[1],
        send_sem=halo_send.at[1],
        recv_sem=halo_recv.at[1],
        device_id={"gx": left},
        device_id_type=MESH,
    )
    def cast(field, x):
        low[field : field + 3, pl.ds(x, 1)] = ext[
            field : field + 3, pl.ds(x + WIDTH, 1)
        ].astype(jnp.bfloat16)

    def cast_adjoint(x, carry):
        cast(3, x)
        return carry

    def cast_base(x, carry):
        cast(0, x)
        return carry

    for q in order:
        adjoint_loads[q].wait()
        lax.fori_loop(q * step, (q + 1) * step, cast_adjoint, 0)
        if q == order[0]:
            pl.semaphore_wait(barrier, 4)
            for load in loads:
                load.start()
        to_partner(q).start()
    loads[0].wait()
    lax.fori_loop(0, cells, cast_base, 0)
    to_right.start()
    to_left.start()
    for q in order:
        to_sibling(q).start()
        base_to_sibling(q).start()
    own_adjoint.start()
    own_base.start()

    def derive(x, carry):
        for half in range(rows // LANES):
            cols = slice(half * LANES, (half + 1) * LANES)

            def plane(f, offset):
                return ext[f, x + (WIDTH + offset), :, cols]

            stream = plane(0, 0)
            across = plane(2, 0)
            couple_x = None
            couple_z = None
            parts = []
            for j in range(3):
                adj = plane(3 + j, 0)
                slope_x = None
                curve = (2.0 * C_CENTER) * adj
                slope_z = None
                base_x = None
                base_z = None
                field = plane(j, 0)
                for k in range(1, WIDTH + 1):
                    a_up, a_down = plane(3 + j, k), plane(3 + j, -k)
                    z_up = pltpu.roll(adj, span - k, 0)
                    z_down = pltpu.roll(adj, k, 0)
                    dx = C_FIRST[k - 1] * (a_up - a_down)
                    dz = C_FIRST[k - 1] * (z_up - z_down)
                    curve = curve + C_SECOND[k - 1] * ((a_up + a_down) + (z_up + z_down))
                    bx = C_FIRST[k - 1] * (plane(j, k) - plane(j, -k))
                    bz = C_FIRST[k - 1] * (
                        pltpu.roll(field, span - k, 0) - pltpu.roll(field, k, 0)
                    )
                    slope_x = dx if slope_x is None else slope_x + dx
                    slope_z = dz if slope_z is None else slope_z + dz
                    base_x = bx if base_x is None else base_x + bx
                    base_z = bz if base_z is None else base_z + bz
                base_x, base_z = adj * base_x, adj * base_z
                couple_x = base_x if couple_x is None else couple_x + base_x
                couple_z = base_z if couple_z is None else couple_z + base_z
                carried = stream * slope_x + across * slope_z + VISCOSITY * curve
                parts.append(adj + STEP_WEIGHT * carried)
            out_ref[0, x, :, cols] = parts[0] - STEP_WEIGHT * couple_x
            out_ref[1, x, :, cols] = parts[1]
            out_ref[2, x, :, cols] = parts[2] - STEP_WEIGHT * couple_z
        return carry

    tall = 3 * step * span
    contract = (((1,), (1,)), ((), ()))

    def product(values, matrix):
        return lax.dot_general(
            values.reshape(tall, values.shape[3]),
            matrix,
            contract,
            preferred_element_type=jnp.float32,
        ).reshape(3, step, span, rows)

    def couple(q, cols, which):
        slopes = product(base_lines[:, layers(q)], chip_first[which])
        there = lines[:, layers(q), :, cols].astype(jnp.float32)
        return there[0] * slopes[0] + there[1] * slopes[1] + there[2] * slopes[2]

    def advance(q):
        lax.fori_loop(q * step, q * step + step, derive, 0)
        base_to_sibling(q).wait_recv()
        to_partner(q).wait_recv()
        forward(q).start()
        part_out[layers(q)] = couple(q, across_y, 1).astype(jnp.bfloat16)
        part_copy(q).start()

    def store(j, q):
        return pltpu.make_async_copy(
            out_ref.at[j, layers(q)], out_hbm.at[j, layers(q)], out_sem.at[j, q]
        )

    place = me * rows + lax.broadcasted_iota(jnp.int32, (step, span, rows), 2)
    inside = (place > 0) & (place < groups * rows - 1)

    def wall(q):
        to_sibling(q).wait_recv()
        forward(q).wait_recv()
        here_x = layers(q)
        slopes = product(lines[:, here_x], first[...])
        curves = product(lines[:, here_x], second[...])
        normal = low[1, here_x].astype(jnp.float32)
        own = couple(q, mine, 0)
        for j in range(3):
            part = normal * slopes[j] + VISCOSITY * curves[j]
            if j == 1:
                part = part - own
            value = out_ref[j, here_x] + STEP_WEIGHT * part
            out_ref[j, here_x] = value if j == 1 else jnp.where(inside, value, 0.0)
            if j != 1:
                store(j, q).start()

    def finish(q, carry):
        part_copy(q).wait_recv()
        value = out_ref[1, layers(q)] - STEP_WEIGHT * part_in[layers(q)].astype(jnp.float32)
        out_ref[1, layers(q)] = jnp.where(inside, value, 0.0)
        store(1, q).start()
        return carry

    for load in loads[1:]:
        load.wait()
    own_adjoint.wait()
    own_base.wait()
    advance(1)

    def interior(q, carry):
        advance(q)
        wall(q - 1)
        return carry

    lax.fori_loop(2, chunks - 1, interior, 0)

    to_right.wait()
    to_left.wait()

    def widen(k, carry):
        ext[:, pl.ds(k, 1)] = halo[0, :, pl.ds(k, 1)].astype(jnp.float32)
        ext[:, pl.ds(k + WIDTH + cells, 1)] = halo[1, :, pl.ds(k, 1)].astype(jnp.float32)
        return carry

    lax.fori_loop(0, WIDTH, widen, 0)

    def edges(k, carry):
        q = k * (chunks - 1)
        advance(q)
        wall((1 - k) * (chunks - 2))
        return carry

    lax.fori_loop(0, 2, edges, 0)
    lax.fori_loop(1, chunks - 1, finish, 0)
    wall(chunks - 1)
    finish(0, 0)
    finish(chunks - 1, 0)

    for q in range(chunks):
        for copy in (to_partner, to_sibling, base_to_sibling, forward, part_copy):
            copy(q).wait_send()
        for j in range(3):
            store(j, q).wait()


def hand_on(source, target, held, sems):
    half = source.shape[1] // 2
    pieces = []
    for j in range(3):
        for h in range(2):
            part = pl.ds(h * half, half)
            pieces.append(
                (
                    pltpu.make_async_copy(source.at[j, part], held.at[j, part], sems.at[0, j, h]),
                    pltpu.make_async_copy(held.at[j, part], target.at[j, part], sems.at[1, j, h]),
                )
            )
    for arrive, _ in pieces:
        arrive.start()
    for arrive, leave in pieces:
        arrive.wait()
        leave.start()
    for _, leave in pieces:
        leave.wait()


def body(base_flow, adjoint, first_op, second_op):
    _, cells, span, rows = base_flow.shape
    groups = lax.axis_size("gy")
    ring = lax.axis_size("gx")
    chunks = cells // WIDTH
    total = groups * rows
    low = jnp.bfloat16
    dma = pltpu.SemaphoreType.DMA
    updated = pl.pallas_call(
        functools.partial(kernel, groups, ring),
        out_shape=jax.ShapeDtypeStruct(base_flow.shape, jnp.float32),
        in_specs=[pl.BlockSpec(memory_space=pltpu.HBM)] * 4,
        out_specs=pl.BlockSpec(memory_space=pltpu.HBM),
        scratch_shapes=[
            pltpu.VMEM((3, cells, span, rows), jnp.float32),
            pltpu.VMEM((6, cells + 2 * WIDTH, span, rows), jnp.float32),
            pltpu.VMEM((6, cells, span, rows), low),
            pltpu.VMEM((3, cells, span, total), low),
            pltpu.VMEM((3, cells, span, 2 * rows), low),
            pltpu.VMEM((2, 6, WIDTH, span, rows), low),
            pltpu.VMEM((rows, total), low),
            pltpu.VMEM((rows, total), low),
            pltpu.VMEM((2, rows, 2 * rows), low),
            pltpu.VMEM((cells, span, rows), low),
            pltpu.VMEM((cells, span, rows), low),
            dma((5 + chunks,)),
            dma((3, chunks)),
            dma((2,)),
            dma((2,)),
            dma((2,)),
            dma((5, chunks)),
            dma((5, chunks)),
        ],
        compiler_params=pltpu.CompilerParams(
            collective_id=0, has_side_effects=True, vmem_limit_bytes=54 * 1024 * 1024
        ),
    )(base_flow, adjoint, first_op, second_op)
    return pl.pallas_call(
        hand_on,
        out_shape=jax.ShapeDtypeStruct(base_flow.shape, jnp.float32),
        in_specs=[pl.BlockSpec(memory_space=pltpu.HBM)],
        out_specs=pl.BlockSpec(memory_space=pltpu.HBM),
        scratch_shapes=[pltpu.VMEM(base_flow.shape, jnp.float32), dma((2, 3, 2))],
    )(updated)


def solution(mesh):
    return jax.shard_map(
        body,
        mesh=mesh,
        in_specs=(P(None, "gx", None, "gy"), P(None, "gx", None, "gy"), P(), P()),
        out_specs=P(None, "gx", None, "gy"),
        check_vma=False,
    )
```
